256 devices in a mesh: section: 8 (over x, core), dom: 32 (over y, z).
Axes of the slice: x: 4, y: 4, z: 8, core: 2. Of those that a mesh axis runs over, the one named last changes fastest.
Arguments:
- node_latents: bfloat16 [8, 32768, 512], P('section', 'dom'), may hold values from -6 to 6
- edge_latents: bfloat16 [8, 49152, 512], P('section', 'dom'), may hold values from -6 to 6
- entering_nodes: bfloat16 [32768, 512], P('dom'), may hold values from -6 to 6
- entering_edges: bfloat16 [49152, 512], P('dom'), may hold values from -6 to 6
- edge_first: bfloat16 [8, 1536, 512], P('section'), may hold values from -0.15625 to 0.15625
- edge_second: bfloat16 [8, 512, 512], P('section'), may hold values from -0.25 to 0.25
- edge_gain: float32 [8, 512], P('section'), may hold values from 0.1 to 1.9
- node_first: bfloat16 [8, 1024, 512], P('section'), may hold values from -0.1875 to 0.1875
- node_second: bfloat16 [8, 512, 512], P('section'), may hold values from -0.25 to 0.25
- node_gain: float32 [8, 512], P('section'), may hold values from 0.1 to 1.9
- pair_list: int32 [32, 12, 3], P('dom'), may hold values from 0 to 7, as said below
- send_list: int32 [32, 4], P('dom'), may hold values from 0 to 7, as said below
- senders: int32 [49152, 128], P('dom'), may hold values from 0 to 1, as said below
- receivers: int32 [49152, 128], P('dom'), may hold values from 0 to 1, as said below
Outputs:
- final_nodes: bfloat16 [8, 32768, 512], P('section', 'dom')
- final_edges: bfloat16 [8, 49152, 512], P('section', 'dom')
The draws below stay inside these ranges and needn't reach their ends.
Inputs may be any that keep to these rules, and one draw needn't show every extreme that they name: `pair_list`: columns 0 and 2 are node block numbers below 8, column 1 a partner code 0 to 4 (0: sender block on the same partition); every partition lists each code 1 to 4 at least once and names each of its node blocks in column 0 at least once. `send_list`: node block numbers below 8. `senders`: each row has exactly one 1. `receivers`: each row has exactly one 1.
All inputs are finite; a program needn't handle non-finite values.
Results may differ from the reference program's by a relative error of at most 0.0075.
Values may be sent and summed in bfloat16 or wider, within the bound.
A program may use at most 128 MiB of HBM per device.

```python
import jax
import jax.numpy as jnp
from jax import lax

D = 512
BLOCK = 128
NODES_DEV = 1024
EDGE_BLOCKS = 12
NODES = 32768
EDGES = 49152
N_SECTION = 8
N_DOM = 32


def draw_pair_list(key, part):
    blocks = NODES_DEV // BLOCK
    number = 3 * NODES_DEV // (2 * BLOCK)

    def draw_device(device_key):
        key_recv, key_rest, key_order, key_local = jax.random.split(device_key, 4)
        receiver = (jax.random.permutation(key_recv, number) % blocks).astype(jnp.int32)
        others = jax.random.randint(key_rest, (number - 4,), 0, 5).astype(jnp.int32)
        partner_codes = jax.random.permutation(key_order, jnp.concatenate([jnp.arange(1, 5, dtype=jnp.int32), others]))
        local_block = jax.random.randint(key_local, (number,), 0, blocks).astype(jnp.int32)
        return jnp.stack([receiver, partner_codes, local_block], axis=1)
    return jax.vmap(draw_device)(jax.random.split(jax.random.fold_in(key, 5), N_DOM))


def draw_send_list(key, part):
    blocks = NODES_DEV // BLOCK
    chosen = jax.random.randint(jax.random.fold_in(key, 11), (N_DOM, 4), 0, blocks).astype(jnp.int32)
    chosen = chosen.at[0, 0].set(0)
    chosen = chosen.at[N_DOM - 1, 3].set(blocks - 1)
    return chosen


def one_hot_rows(key):
    total = 3 * NODES_DEV // (2 * BLOCK) * BLOCK * N_DOM
    column = jax.random.randint(key, (total,), 0, BLOCK)
    return (column[:, None] == jnp.arange(BLOCK)[None, :]).astype(jnp.int32)


def draw_senders(key, part):
    return one_hot_rows(jax.random.fold_in(key, 21))


def draw_receivers(key, part):
    return one_hot_rows(jax.random.fold_in(key, 22))


def shard_levels(key, dims, pieces, low, high):
    level, own = 1.0, jax.random.fold_in(key, 6)
    for position, shards_of in pieces:
        steps = jnp.exp(jax.random.uniform(jax.random.fold_in(own, position), (shards_of,), jnp.float32, low / len(pieces), high / len(pieces)))
        level = level * jnp.repeat(steps, dims[position] // shards_of).reshape([-1 if axis == position else 1 for axis in range(len(dims))])
    return level


def bell_draw(key, extent, deviation, reach, shards=(), kind=jnp.bfloat16):
    loudness = shard_levels(key, extent, shards, -0.22, 0.18) if shards else 1.0
    values = jax.random.normal(key, extent, jnp.float32) * deviation * loudness
    return jnp.minimum(jnp.maximum(values, -reach), reach).astype(kind)


def setup_inputs(seed: int = 0) -> dict:
    key_list = jax.random.split(jax.random.key(seed), 15)
    return {
        "node_latents": bell_draw(key_list[0], (N_SECTION, NODES, D), 1.0, 6.0, ((0, 8), (1, 32))),
        "edge_latents": bell_draw(key_list[1], (N_SECTION, EDGES, D), 1.0, 6.0, ((0, 8), (1, 32))),
        "entering_nodes": bell_draw(key_list[2], (NODES, D), 1.0, 6.0, ((0, 32),)),
        "entering_edges": bell_draw(key_list[3], (EDGES, D), 1.0, 6.0, ((0, 32),)),
        "edge_first": bell_draw(key_list[4], (N_SECTION, 3 * D, D), (3 * D) ** -0.5, 0.15625, ((0, 8),)),
        "edge_second": bell_draw(key_list[5], (N_SECTION, D, D), D ** -0.5, 0.25, ((0, 8),)),
        "edge_gain": jnp.clip(1.0 + 0.18 * jax.random.normal(key_list[6], (N_SECTION, D), jnp.float32), 0.1, 1.9),
        "node_first": bell_draw(key_list[7], (N_SECTION, 2 * D, D), (2 * D) ** -0.5, 0.1875, ((0, 8),)),
        "node_second": bell_draw(key_list[8], (N_SECTION, D, D), D ** -0.5, 0.25, ((0, 8),)),
        "node_gain": jnp.clip(1.0 + 0.18 * jax.random.normal(key_list[9], (N_SECTION, D), jnp.float32), 0.1, 1.9),
        "pair_list": draw_pair_list(jax.random.fold_in(key_list[14], 71), 0),
        "send_list": draw_send_list(jax.random.fold_in(key_list[14], 71), 0),
        "senders": draw_senders(jax.random.fold_in(key_list[14], 71), 0),
        "receivers": draw_receivers(jax.random.fold_in(key_list[14], 71), 0),
    }


partner_offsets = (1, -1, 2, -2)
epsilon = 1e-05
highest = lax.Precision.HIGHEST

def layer_norm(values, gain):
    centred = values - lax.optimization_barrier(jnp.mean(values, axis=-1, keepdims=True))
    spread = lax.optimization_barrier(jnp.mean(centred * centred, axis=-1, keepdims=True))
    return centred * lax.rsqrt(spread + epsilon) * gain

def product_wide(left, right):
    return jnp.dot(left.astype(jnp.float32), right.astype(jnp.float32), precision=highest)

def batched(form, left, right):
    return jnp.einsum(form, left.astype(jnp.float32), right.astype(jnp.float32), precision=highest)

def selector(index, number):
    return (index[:, None] == jnp.arange(number, dtype=jnp.int32)[None, :]).astype(jnp.float32)

def edge_part(node_rows, edge_rows, incoming, pairs, send_mat, recv_mat, edge_first, edge_second, edge_gain):
    blocks = NODES_DEV // BLOCK
    rows_all = EDGE_BLOCKS * BLOCK
    own_blocks = node_rows.reshape(blocks, BLOCK, D)
    lookup = jnp.concatenate([own_blocks, incoming], axis=0)
    partner_codes = pairs[:, 1]
    source = jnp.where(partner_codes == 0, pairs[:, 2], blocks + partner_codes - 1).astype(jnp.int32)
    sender_blocks = lookup[source]
    receiver_blocks = own_blocks[pairs[:, 0]]
    from_send = batched('kei,kid->ked', send_mat, sender_blocks).astype(jnp.bfloat16)
    from_recv = batched('kei,kid->ked', recv_mat, receiver_blocks).astype(jnp.bfloat16)
    first_layer = product_wide(edge_rows, edge_first[:D])
    first_layer = first_layer + product_wide(from_send.reshape(rows_all, D), edge_first[D:2 * D])
    first_layer = first_layer + product_wide(from_recv.reshape(rows_all, D), edge_first[2 * D:])
    hidden = jnp.maximum(first_layer, 0.0).astype(jnp.bfloat16)
    message = layer_norm(product_wide(hidden, edge_second), edge_gain)
    message_low = message.astype(jnp.bfloat16)
    new_edges = (edge_rows.astype(jnp.float32) + message).astype(jnp.bfloat16)
    blocked = message_low.reshape(EDGE_BLOCKS, BLOCK, D)
    at_send = batched('kei,ked->kid', send_mat, blocked)
    at_recv = batched('kei,ked->kid', recv_mat, blocked)
    block_sums = batched('kn,kbd->nbd', selector(pairs[:, 0], blocks + 4), at_recv)
    block_sums = block_sums + batched('kn,kbd->nbd', selector(source, blocks + 4), at_send)
    return (new_edges, block_sums[:blocks], block_sums[blocks:].astype(jnp.bfloat16))

def node_part(node_rows, own_sums, returned, sends, node_first, node_second, node_gain):
    blocks = NODES_DEV // BLOCK
    gathered = own_sums + batched('jn,jbd->nbd', selector(sends, blocks), returned)
    summed = gathered.reshape(NODES_DEV, D).astype(jnp.bfloat16)
    first_layer = product_wide(node_rows, node_first[:D]) + product_wide(summed, node_first[D:])
    hidden = jnp.maximum(first_layer, 0.0).astype(jnp.bfloat16)
    update = layer_norm(product_wide(hidden, node_second), node_gain)
    return (node_rows.astype(jnp.float32) + update).astype(jnp.bfloat16)

def whole_layer(nodes, edges, weights, pair_list, send_list, send_mats, recv_mats):
    edge_first, edge_second, edge_gain, node_first, node_second, node_gain = weights
    blocks = NODES_DEV // BLOCK
    own = nodes.reshape(N_DOM, blocks, BLOCK, D)
    outgoing = jax.vmap(lambda blocks_of, chosen: blocks_of[chosen])(own, send_list)
    incoming = jnp.stack([jnp.roll(outgoing[:, offset_slot], partner_offsets[offset_slot], axis=0) for offset_slot in range(4)], axis=1)
    new_edges, own_sums, partials = jax.vmap(edge_part, in_axes=(0, 0, 0, 0, 0, 0, None, None, None))(nodes, edges, incoming, pair_list, send_mats, recv_mats, edge_first, edge_second, edge_gain)
    returned = jnp.stack([jnp.roll(partials[:, offset_slot], -partner_offsets[offset_slot], axis=0) for offset_slot in range(4)], axis=1)
    new_nodes = jax.vmap(node_part, in_axes=(0, 0, 0, 0, None, None, None))(nodes, own_sums, returned, send_list, node_first, node_second, node_gain)
    return (new_nodes, new_edges)

def reference(node_latents, edge_latents, entering_nodes, entering_edges, edge_first, edge_second, edge_gain, node_first, node_second, node_gain, pair_list, send_list, senders, receivers):
    edge_count = EDGE_BLOCKS * BLOCK
    send_mats = senders.reshape(N_DOM, EDGE_BLOCKS, BLOCK, BLOCK)
    recv_mats = receivers.reshape(N_DOM, EDGE_BLOCKS, BLOCK, BLOCK)

    def run_layer(section, nodes, edges):
        weights = (edge_first[section], edge_second[section], edge_gain[section], node_first[section], node_second[section], node_gain[section])
        new_nodes, new_edges = whole_layer(nodes.reshape(N_DOM, NODES_DEV, D), edges.reshape(N_DOM, edge_count, D), weights, pair_list, send_list, send_mats, recv_mats)
        return (new_nodes.reshape(NODES, D), new_edges.reshape(EDGES, D))
    ticked = [run_layer(section, node_latents[section], edge_latents[section]) for section in range(N_SECTION)]
    inputs = [(entering_nodes, entering_edges)] + ticked[:-1]
    results = [run_layer(section, inputs[section][0], inputs[section][1]) for section in range(N_SECTION)]
    final_nodes = jnp.stack([entry[0] for entry in results], axis=0)
    final_edges = jnp.stack([entry[1] for entry in results], axis=0)
    return (final_nodes, final_edges)
```

```python
import functools

import jax
import jax.numpy as jnp
from jax import lax
from jax.experimental import pallas as pl
from jax.experimental.pallas import tpu as pltpu
from jax.sharding import PartitionSpec as P

OFFSETS = (1, -1, 2, -2)
EPSILON = 1e-05
MESH = pl.DeviceIdType.MESH
BF16 = jnp.bfloat16
F32 = jnp.float32
B = 128
ROWS = 256


def product(left, right):
    return jnp.dot(left, right, preferred_element_type=F32)


def layer_norm(values, gain):
    centred = values - jnp.mean(values, axis=-1, keepdims=True)
    spread = jnp.mean(centred * centred, axis=-1, keepdims=True)
    return centred * lax.rsqrt(spread + EPSILON) * gain


def blocks_of(step):
    return pl.ds(step * (ROWS // B), ROWS // B)


def flat(blocks):
    return blocks.reshape(blocks.shape[0] * blocks.shape[1], blocks.shape[2])


def split(rows):
    return rows.reshape(rows.shape[0] // B, B, rows.shape[1])


def rows_of(step, size=ROWS):
    return pl.ds(pl.multiple_of(step * size, size), size)


def kernel(
    n_sec, n_dom,
    nl, el, en, ee, wef_h, wes_h, ge, wnf_h, wns_h, gn, pairs, sends, snd_h, rcv_h,
    fn, fe,
    x0, e0, x1, e1, xo, eo, xf, ef, wef, wes, wnf, wns, snd, rcv,
    gsr, scat, look, pr, ew, xn, msg, own,
    stage0, stage1, inc0, inc1, part0, part1, ret0, ret1,
    load_sem, ent_sem, out_sem_x, out_sem_e,
    a_send, a_recv, c_send, c_recv, x_send, x_recv, e_send, e_recv,
):
    D = x0.shape[2]
    nb = x0.shape[0]
    kb = e0.shape[0] // B
    x_steps = x0.shape[0] * B // ROWS
    e_steps = e0.shape[0] // ROWS
    sec = lax.axis_index("section")
    dom = lax.axis_index("dom")
    nxt = lax.rem(sec + 1, n_sec)
    prv = lax.rem(sec + n_sec - 1, n_sec)

    loads = {}
    for i, (name, src, dst) in enumerate((
        ("x", nl, x0), ("wef", wef_h.at[0], wef), ("snd", snd_h, snd), ("rcv", rcv_h, rcv),
        ("e", el.at[0], e0), ("wes", wes_h.at[0], wes), ("wnf", wnf_h.at[0], wnf), ("wns", wns_h.at[0], wns),
    )):
        loads[name] = pltpu.make_async_copy(src, dst, load_sem.at[i])
        loads[name].start()
    enter_x = pltpu.make_async_copy(en, x1, ent_sem.at[0])
    enter_e = pltpu.make_async_copy(ee, e1, ent_sem.at[1])

    @pl.when(sec == 0)
    def _():
        enter_x.start()
        enter_e.start()

    barrier = pltpu.get_barrier_semaphore()
    for o in OFFSETS:
        pl.semaphore_signal(barrier, inc=1, device_id=(sec, lax.rem(dom + o + n_dom, n_dom)), device_id_type=MESH)
    pl.semaphore_signal(barrier, inc=1, device_id=(nxt, dom), device_id_type=MESH)
    pl.semaphore_signal(barrier, inc=1, device_id=(prv, dom), device_id_type=MESH)

    def forth(t, c):
        stage, inc = ((stage0, inc0), (stage1, inc1))[t]
        return pltpu.make_async_remote_copy(
            stage.at[c], inc.at[c], a_send.at[t, c], a_recv.at[t, c],
            device_id=(sec, lax.rem(dom + OFFSETS[c] + n_dom, n_dom)), device_id_type=MESH)

    def back(t, c):
        part, ret = ((part0, ret0), (part1, ret1))[t]
        return pltpu.make_async_remote_copy(
            part.at[c], ret.at[c], c_send.at[t, c], c_recv.at[t, c],
            device_id=(sec, lax.rem(dom - OFFSETS[c] + n_dom, n_dom)), device_id_type=MESH)

    def next_x(i):
        return pltpu.make_async_remote_copy(
            xo.at[blocks_of(i)], x1.at[blocks_of(i)], x_send.at[i], x_recv.at[i],
            device_id=(nxt, dom), device_id_type=MESH)

    def next_e(i):
        return pltpu.make_async_remote_copy(
            eo.at[rows_of(i)], e1.at[rows_of(i)], e_send.at[i], e_recv.at[i],
            device_id=(nxt, dom), device_id_type=MESH)

    def out_x(i):
        return pltpu.make_async_copy(xf.at[blocks_of(i)], fn.at[blocks_of(i)], out_sem_x.at[i])

    def out_e(i):
        return pltpu.make_async_copy(ef.at[rows_of(i)], fe.at[0, rows_of(i)], out_sem_e.at[i])

    def source(k):
        code = pairs[0, k, 1]
        return jnp.where(code == 0, pairs[0, k, 2], nb + code - 1)

    def send_blocks(t, x):
        for c in range(4):
            (stage0, stage1)[t][c] = x[sends[0, c]]
            forth(t, c).start()

    def tick(t, x, e, wait_e):
        last = t == 1
        inc = (inc0, inc1)[t]
        part = (part0, part1)[t]
        ret = (ret0, ret1)[t]
        x_new = (xo, xf)[t]
        e_new = (eo, ef)[t]

        def pre(i, _):
            r = blocks_of(i)
            xb = flat(x[r])
            look[r] = split(product(xb, wef[D : 2 * D, :]).astype(BF16))
            pr[r] = split(product(xb, wef[2 * D :, :]).astype(BF16))
            return 0

        lax.fori_loop(0, x_steps, pre, 0)
        wait_e()

        def edge_pre(i, _):
            r = rows_of(i)
            ew[r, :] = product(e[r, :], wef[0:D, :])
            return 0

        lax.fori_loop(0, e_steps, edge_pre, 0)
        if not last:
            loads["wnf"].wait()

        def node_pre(i, _):
            r = rows_of(i)
            xn[r, :] = product(flat(x[blocks_of(i)]), wnf[0:D, :])
            return 0

        lax.fori_loop(0, x_steps, node_pre, 0)
        if not last:
            loads["wes"].wait()
            loads["wns"].wait()
        for c in range(4):
            forth(t, c).wait_recv()
        for c in range(0, 4, 2):
            both = flat(inc[c : c + 2])
            look[nb + c : nb + c + 2] = split(product(both, wef[D : 2 * D, :]).astype(BF16))

        def edge(i, _):
            parts = []
            for j in range(ROWS // B):
                k = i * (ROWS // B) + j
                kr = rows_of(k, B)
                src = source(k)
                rcvb = pairs[0, k, 0]
                feats = jnp.concatenate([look[src], pr[rcvb]], axis=0)
                pre_act = ew[kr, :] + product(gsr[kr, :], feats)
                parts.append(jnp.maximum(pre_act, 0.0).astype(BF16))
            r = rows_of(i)
            message = layer_norm(product(jnp.concatenate(parts, axis=0), wes[...]), ge[...])
            msg[r, :] = message.astype(BF16)
            e_new[r, :] = (e[r, :].astype(F32) + message).astype(BF16)
            if last:
                out_e(i).start()
            else:
                @pl.when(sec < n_sec - 1)
                def _():
                    next_e(i).start()
            return 0

        lax.fori_loop(0, e_steps, edge, 0)
        for c in range(0, 4, 2):
            sums = product(scat[(nb + c) * B : (nb + c + 2) * B, :], msg[...]).astype(BF16)
            part[c] = sums[:B]
            part[c + 1] = sums[B:]
            back(t, c).start()
            back(t, c + 1).start()

        def own_sum(i, _):
            r = rows_of(i)
            own[r, :] = product(scat[r, :], msg[...])
            return 0

        lax.fori_loop(0, x_steps, own_sum, 0)
        for c in range(4):
            back(t, c).wait_recv()

        def node(i, _):
            r = rows_of(i)
            sums = []
            for j in range(ROWS // B):
                n = i * (ROWS // B) + j
                total = own[rows_of(n, B), :]
                for c in range(4):
                    total = total + jnp.where(sends[0, c] == n, 1.0, 0.0) * ret[c].astype(F32)
                sums.append(total.astype(BF16))
            agg = jnp.concatenate(sums, axis=0)
            hidden = jnp.maximum(xn[r, :] + product(agg, wnf[D:, :]), 0.0).astype(BF16)
            update = layer_norm(product(hidden, wns[...]), gn[...])
            x_new[blocks_of(i)] = split((flat(x[blocks_of(i)]).astype(F32) + update).astype(BF16))
            if last:
                out_x(i).start()
            else:
                @pl.when(sec < n_sec - 1)
                def _():
                    next_x(i).start()
            return 0

        lax.fori_loop(0, x_steps, node, 0)

    pl.semaphore_wait(barrier, 6)
    loads["x"].wait()
    send_blocks(0, x0)
    loads["snd"].wait()
    loads["rcv"].wait()

    def build(k, _):
        kr = rows_of(k, B)
        s_mat = snd[kr, :].astype(F32)
        r_mat = rcv[kr, :].astype(F32)
        gsr[kr, 0:B] = s_mat.astype(BF16)
        gsr[kr, B : 2 * B] = r_mat.astype(BF16)
        s_t = s_mat.T
        r_t = r_mat.T
        src = source(k)
        rcvb = pairs[0, k, 0]
        for n in range(nb + 4):
            block = s_t * jnp.where(src == n, 1.0, 0.0)
            if n < nb:
                block = block + r_t * jnp.where(rcvb == n, 1.0, 0.0)
            scat[n * B : (n + 1) * B, kr] = block.astype(BF16)
        return 0

    lax.fori_loop(0, kb, build, 0)
    loads["wef"].wait()
    tick(0, x0, e0, lambda: loads["e"].wait())

    @pl.when(sec == 0)
    def _():
        enter_x.wait()

    @pl.when(sec > 0)
    def _():
        for i in range(x_steps):
            next_x(i).wait_recv()

    send_blocks(1, x1)

    def wait_e1():
        @pl.when(sec == 0)
        def _():
            enter_e.wait()

        @pl.when(sec > 0)
        def _():
            for i in range(e_steps):
                next_e(i).wait_recv()

    tick(1, x1, e1, wait_e1)

    for i in range(x_steps):
        out_x(i).wait()
    for i in range(e_steps):
        out_e(i).wait()
    for t in range(2):
        for c in range(4):
            forth(t, c).wait_send()
            back(t, c).wait_send()

    @pl.when(sec < n_sec - 1)
    def _():
        for i in range(x_steps):
            next_x(i).wait_send()
        for i in range(e_steps):
            next_e(i).wait_send()


def local(n_sec, n_dom, *args):
    nl, el = args[0], args[1]
    n_rows, D = nl.shape[1:]
    e_rows = el.shape[1]
    nb = n_rows // B
    any_space = pl.BlockSpec(memory_space=pl.ANY)
    vmem = pl.BlockSpec(memory_space=pltpu.VMEM)
    smem = pl.BlockSpec(memory_space=pltpu.SMEM)
    specs = [any_space] * 14
    specs[6] = specs[9] = vmem
    specs[10] = specs[11] = smem
    nodes = pltpu.VMEM((nb, B, D), BF16)
    edges = pltpu.VMEM((e_rows, D), BF16)
    slots = pltpu.VMEM((4, B, D), BF16)
    dma = pltpu.SemaphoreType.DMA
    x_steps, e_steps = n_rows // ROWS, e_rows // ROWS
    args = (nl.reshape(nb, B, D), args[1], args[2].reshape(nb, B, D)) + args[3:]
    final_nodes, final_edges = pl.pallas_call(
        functools.partial(kernel, n_sec, n_dom),
        out_shape=(jax.ShapeDtypeStruct((nb, B, D), BF16), jax.ShapeDtypeStruct(el.shape, BF16)),
        in_specs=specs,
        out_specs=(any_space, any_space),
        scratch_shapes=[
            nodes, edges, nodes, edges, nodes, edges, nodes, edges,
            pltpu.VMEM((3 * D, D), BF16), pltpu.VMEM((D, D), BF16),
            pltpu.VMEM((2 * D, D), BF16), pltpu.VMEM((D, D), BF16),
            pltpu.VMEM((e_rows, B), jnp.int32), pltpu.VMEM((e_rows, B), jnp.int32),
            pltpu.VMEM((e_rows, 2 * B), BF16),
            pltpu.VMEM(((nb + 4) * B, e_rows), BF16),
            pltpu.VMEM((nb + 4, B, D), BF16),
            nodes,
            pltpu.VMEM((e_rows, D), F32),
            pltpu.VMEM((n_rows, D), F32),
            edges,
            pltpu.VMEM((n_rows, D), F32),
            slots, slots, slots, slots, slots, slots, slots, slots,
            dma((8,)), dma((2,)), dma((x_steps,)), dma((e_steps,)),
            dma((2, 4)), dma((2, 4)), dma((2, 4)), dma((2, 4)),
            dma((x_steps,)), dma((x_steps,)), dma((e_steps,)), dma((e_steps,)),
        ],
        compiler_params=pltpu.CompilerParams(
            collective_id=0, has_side_effects=True, vmem_limit_bytes=56 << 20),
    )(*args)
    return final_nodes.reshape(nl.shape), final_edges


def solution(mesh):
    placed = (
        P("section", "dom", None),
        P("section", "dom", None),
        P("dom", None),
        P("dom", None),
        P("section", None, None),
        P("section", None, None),
        P("section", None),
        P("section", None, None),
        P("section", None, None),
        P("section", None),
        P("dom", None, None),
        P("dom", None),
        P("dom", None),
        P("dom", None),
    )
    return jax.shard_map(
        functools.partial(local, mesh.shape["section"], mesh.shape["dom"]),
        mesh=mesh,
        in_specs=placed,
        out_specs=(P("section", "dom", None), P("section", "dom", None)),
        check_vma=False,
    )
```

```python
import functools

import jax
import jax.numpy as jnp
from jax import lax
from jax.experimental import pallas as pl
from jax.experimental.pallas import tpu as pltpu
from jax.sharding import PartitionSpec as P

OFFSETS = (1, -1, 2, -2)
EPSILON = 1e-05
MESH = pl.DeviceIdType.MESH
BF16 = jnp.bfloat16
F32 = jnp.float32
B = 128
ROWS = 256


def product(left, right):
    return jnp.dot(left, right, preferred_element_type=F32)


def layer_norm(values, gain):
    centred = values - jnp.mean(values, axis=-1, keepdims=True)
    spread = jnp.mean(centred * centred, axis=-1, keepdims=True)
    return centred * lax.rsqrt(spread + EPSILON) * gain


def blocks_of(step):
    return pl.ds(step * (ROWS // B), ROWS // B)


def flat(blocks):
    return blocks.reshape(blocks.shape[0] * blocks.shape[1], blocks.shape[2])


def split(rows):
    return rows.reshape(rows.shape[0] // B, B, rows.shape[1])


def rows_of(step, size=ROWS):
    return pl.ds(pl.multiple_of(step * size, size), size)


def kernel(
    n_sec, n_dom,
    nl, el, en, ee, wef_h, wes_h, ge, wnf_h, wns_h, gn, pairs, sends, snd_h, rcv_h,
    fn, fe,
    x0, e0, x1, e1, xo, eo, xf, ef, wef, wes, wnf, wns, snd, rcv,
    gsr, scat, look, pr, ew, xn, msg, own,
    stage0, stage1, inc0, inc1, part0, part1, ret0, ret1,
    go_sem, load_sem, ent_sem, out_sem_x, out_sem_e,
    a_send, a_recv, c_send, c_recv, x_send, x_recv, e_send, e_recv,
):
    D = x0.shape[2]
    nb = x0.shape[0]
    kb = e0.shape[0] // B
    x_steps = x0.shape[0] * B // ROWS
    e_steps = e0.shape[0] // ROWS
    sec = lax.axis_index("section")
    dom = lax.axis_index("dom")
    nxt = lax.rem(sec + 1, n_sec)
    prv = lax.rem(sec + n_sec - 1, n_sec)
    ahead = lax.rem(sec, 2) == 1
    early = 2 * e_steps // 3

    loads = {}
    for i, (name, src, dst) in enumerate((
        ("x", nl, x0), ("wef", wef_h.at[0], wef), ("snd", snd_h, snd), ("rcv", rcv_h, rcv),
        ("e", el.at[0], e0), ("wes", wes_h.at[0], wes), ("wnf", wnf_h.at[0], wnf), ("wns", wns_h.at[0], wns),
    )):
        loads[name] = pltpu.make_async_copy(src, dst, load_sem.at[i])
        loads[name].start()
    enter_x = pltpu.make_async_copy(en, x1, ent_sem.at[0])
    enter_e = pltpu.make_async_copy(ee, e1, ent_sem.at[1])

    @pl.when(sec == 0)
    def _():
        enter_x.start()
        enter_e.start()

    barrier = pltpu.get_barrier_semaphore()
    for o in OFFSETS:
        pl.semaphore_signal(barrier, inc=1, device_id=(sec, lax.rem(dom + o + n_dom, n_dom)), device_id_type=MESH)
    pl.semaphore_signal(barrier, inc=1, device_id=(nxt, dom), device_id_type=MESH)
    pl.semaphore_signal(barrier, inc=1, device_id=(prv, dom), device_id_type=MESH)

    def forth(t, c):
        stage, inc = ((stage0, inc0), (stage1, inc1))[t]
        return pltpu.make_async_remote_copy(
            stage.at[c], inc.at[c], a_send.at[t, c], a_recv.at[t, c],
            device_id=(sec, lax.rem(dom + OFFSETS[c] + n_dom, n_dom)), device_id_type=MESH)

    def back(t, c):
        part, ret = ((part0, ret0), (part1, ret1))[t]
        return pltpu.make_async_remote_copy(
            part.at[c], ret.at[c], c_send.at[t, c], c_recv.at[t, c],
            device_id=(sec, lax.rem(dom - OFFSETS[c] + n_dom, n_dom)), device_id_type=MESH)

    def next_x(i):
        return pltpu.make_async_remote_copy(
            xo.at[blocks_of(i)], x1.at[blocks_of(i)], x_send.at[i], x_recv.at[i],
            device_id=(nxt, dom), device_id_type=MESH)

    def next_e(i):
        return pltpu.make_async_remote_copy(
            eo.at[rows_of(i)], e1.at[rows_of(i)], e_send.at[i], e_recv.at[i],
            device_id=(nxt, dom), device_id_type=MESH)

    def out_x(i):
        return pltpu.make_async_copy(xf.at[blocks_of(i)], fn.at[blocks_of(i)], out_sem_x.at[i])

    def out_e(i):
        return pltpu.make_async_copy(ef.at[rows_of(i)], fe.at[0, rows_of(i)], out_sem_e.at[i])

    def source(k):
        code = pairs[1, 0, k]
        return jnp.where(code == 0, pairs[2, 0, k], nb + code - 1)

    def send_blocks(t, x):
        for c in range(4):
            (stage0, stage1)[t][c] = x[sends[0, c]]
            forth(t, c).start()

    def tick(t, x, e, ready_x, ready_e):
        last = t == 1
        inc = (inc0, inc1)[t]
        part = (part0, part1)[t]
        ret = (ret0, ret1)[t]
        x_new = (xo, xf)[t]
        e_new = (eo, ef)[t]

        def pre(i, _):
            ready_x(i)
            r = blocks_of(i)
            xb = flat(x[r])
            look[r] = split(product(xb, wef[D : 2 * D, :]).astype(BF16))
            pr[r] = split(product(xb, wef[2 * D :, :]).astype(BF16))
            return 0

        lax.fori_loop(0, x_steps, pre, 0, unroll=True)
        if t == 0:
            loads["e"].wait()

            @pl.when(ahead)
            def _():
                for c in range(4):
                    forth(0, c).wait_send()
                pl.semaphore_signal(go_sem, inc=1, device_id=(sec - 1, dom), device_id_type=MESH)

            @pl.when(jnp.logical_not(ahead))
            def _():
                pl.semaphore_wait(go_sem, 1)
                send_blocks(0, x0)
        else:
            send_blocks(1, x1)

        def edge_pre(i, _):
            ready_e(i)
            r = rows_of(i)
            ew[r, :] = product(e[r, :], wef[0:D, :])
            return 0

        lax.fori_loop(0, e_steps, edge_pre, 0, unroll=True)
        if not last:
            loads["wes"].wait()
            loads["wns"].wait()
        for c in range(4):
            forth(t, c).wait_recv()
        for c in range(0, 4, 2):
            both = flat(inc[c : c + 2])
            look[nb + c : nb + c + 2] = split(product(both, wef[D : 2 * D, :]).astype(BF16))

        def edge(i, _):
            parts = []
            for j in range(ROWS // B):
                k = i * (ROWS // B) + j
                kr = rows_of(k, B)
                src = source(k)
                rcvb = pairs[0, 0, k]
                feats = jnp.concatenate([look[src], pr[rcvb]], axis=0)
                pre_act = ew[kr, :] + product(gsr[kr, :], feats)
                parts.append(jnp.maximum(pre_act, 0.0).astype(BF16))
            r = rows_of(i)
            message = layer_norm(product(jnp.concatenate(parts, axis=0), wes[...]), ge[...])
            msg[r, :] = message.astype(BF16)
            e_new[r, :] = (e[r, :].astype(F32) + message).astype(BF16)
            if last:
                out_e(i).start()
            else:
                @pl.when(jnp.logical_and(sec < n_sec - 1, i < early))
                def _():
                    next_e(i).start()
            return 0

        lax.fori_loop(0, e_steps, edge, 0, unroll=True)
        for c in range(0, 4, 2):
            sums = product(scat[(nb + c) * B : (nb + c + 2) * B, :], msg[...]).astype(BF16)
            part[c] = sums[:B]
            part[c + 1] = sums[B:]
            back(t, c).start()
            back(t, c + 1).start()

        def own_sum(i, _):
            r = rows_of(i)
            own[r, :] = product(scat[r, :], msg[...])
            return 0

        lax.fori_loop(0, x_steps, own_sum, 0, unroll=True)
        if not last:
            loads["wnf"].wait()

        def node_pre(i, _):
            r = rows_of(i)
            xn[r, :] = product(flat(x[blocks_of(i)]), wnf[0:D, :])
            return 0

        lax.fori_loop(0, x_steps, node_pre, 0, unroll=True)
        for c in range(4):
            back(t, c).wait_recv()

        def node(i, _):
            r = rows_of(i)
            sums = []
            for j in range(ROWS // B):
                n = i * (ROWS // B) + j
                total = own[rows_of(n, B), :]
                for c in range(4):
                    total = total + jnp.where(sends[0, c] == n, 1.0, 0.0) * ret[c].astype(F32)
                sums.append(total.astype(BF16))
            agg = jnp.concatenate(sums, axis=0)
            hidden = jnp.maximum(xn[r, :] + product(agg, wnf[D:, :]), 0.0).astype(BF16)
            update = layer_norm(product(hidden, wns[...]), gn[...])
            x_new[blocks_of(i)] = split((flat(x[blocks_of(i)]).astype(F32) + update).astype(BF16))
            if last:
                out_x(i).start()
            else:
                @pl.when(sec < n_sec - 1)
                def _():
                    next_x(i).start()
            return 0

        lax.fori_loop(0, x_steps, node, 0, unroll=True)
        if not last:
            @pl.when(sec < n_sec - 1)
            def _():
                for i in range(early, e_steps):
                    next_e(i).start()

    pl.semaphore_wait(barrier, 6)
    loads["x"].wait()

    @pl.when(ahead)
    def _():
        send_blocks(0, x0)

    loads["snd"].wait()
    loads["rcv"].wait()

    def build(k, _):
        kr = rows_of(k, B)
        s_mat = snd[kr, :].astype(F32)
        r_mat = rcv[kr, :].astype(F32)
        gsr[kr, 0:B] = s_mat.astype(BF16)
        gsr[kr, B : 2 * B] = r_mat.astype(BF16)
        s_t = s_mat.T
        r_t = r_mat.T
        src = source(k)
        rcvb = pairs[0, 0, k]
        for n in range(nb + 4):
            block = s_t * jnp.where(src == n, 1.0, 0.0)
            if n < nb:
                block = block + r_t * jnp.where(rcvb == n, 1.0, 0.0)
            scat[n * B : (n + 1) * B, kr] = block.astype(BF16)
        return 0

    lax.fori_loop(0, kb, build, 0)
    loads["wef"].wait()
    tick(0, x0, e0, lambda i: None, lambda i: None)

    @pl.when(sec == 0)
    def _():
        enter_x.wait()
        enter_e.wait()

    def ready_x(i):
        @pl.when(sec > 0)
        def _():
            next_x(i).wait_recv()

    def ready_e(i):
        @pl.when(sec > 0)
        def _():
            next_e(i).wait_recv()

    tick(1, x1, e1, ready_x, ready_e)

    for i in range(x_steps):
        out_x(i).wait()
    for i in range(e_steps):
        out_e(i).wait()
    for c in range(4):
        forth(1, c).wait_send()
        back(0, c).wait_send()
        back(1, c).wait_send()

    @pl.when(jnp.logical_not(ahead))
    def _():
        for c in range(4):
            forth(0, c).wait_send()

    @pl.when(sec < n_sec - 1)
    def _():
        for i in range(x_steps):
            next_x(i).wait_send()
        for i in range(e_steps):
            next_e(i).wait_send()


def local(n_sec, n_dom, *args):
    nl, el = args[0], args[1]
    n_rows, D = nl.shape[1:]
    e_rows = el.shape[1]
    nb = n_rows // B
    any_space = pl.BlockSpec(memory_space=pl.ANY)
    vmem = pl.BlockSpec(memory_space=pltpu.VMEM)
    smem = pl.BlockSpec(memory_space=pltpu.SMEM)
    specs = [any_space] * 14
    specs[6] = specs[9] = vmem
    specs[10] = specs[11] = smem
    nodes = pltpu.VMEM((nb, B, D), BF16)
    edges = pltpu.VMEM((e_rows, D), BF16)
    slots = pltpu.VMEM((4, B, D), BF16)
    dma = pltpu.SemaphoreType.DMA
    x_steps, e_steps = n_rows // ROWS, e_rows // ROWS
    pairs = jnp.transpose(args[10], (2, 0, 1))
    args = (nl.reshape(nb, B, D), args[1], args[2].reshape(nb, B, D)) + args[3:10] + (pairs,) + args[11:]
    final_nodes, final_edges = pl.pallas_call(
        functools.partial(kernel, n_sec, n_dom),
        out_shape=(jax.ShapeDtypeStruct((nb, B, D), BF16), jax.ShapeDtypeStruct(el.shape, BF16)),
        in_specs=specs,
        out_specs=(any_space, any_space),
        scratch_shapes=[
            nodes, edges, nodes, edges, nodes, edges, nodes, edges,
            pltpu.VMEM((3 * D, D), BF16), pltpu.VMEM((D, D), BF16),
            pltpu.VMEM((2 * D, D), BF16), pltpu.VMEM((D, D), BF16),
            pltpu.VMEM((e_rows, B), jnp.int32), pltpu.VMEM((e_rows, B), jnp.int32),
            pltpu.VMEM((e_rows, 2 * B), BF16),
            pltpu.VMEM(((nb + 4) * B, e_rows), BF16),
            pltpu.VMEM((nb + 4, B, D), BF16),
            nodes,
            pltpu.VMEM((e_rows, D), F32),
            pltpu.VMEM((n_rows, D), F32),
            edges,
            pltpu.VMEM((n_rows, D), F32),
            slots, slots, slots, slots, slots, slots, slots, slots,
            pltpu.SemaphoreType.REGULAR, dma((8,)), dma((2,)), dma((x_steps,)), dma((e_steps,)),
            dma((2, 4)), dma((2, 4)), dma((2, 4)), dma((2, 4)),
            dma((x_steps,)), dma((x_steps,)), dma((e_steps,)), dma((e_steps,)),
        ],
        compiler_params=pltpu.CompilerParams(
            collective_id=0, has_side_effects=True, vmem_limit_bytes=56 << 20),
    )(*args)
    return final_nodes.reshape(nl.shape), final_edges


def solution(mesh):
    placed = (
        P("section", "dom", None),
        P("section", "dom", None),
        P("dom", None),
        P("dom", None),
        P("section", None, None),
        P("section", None, None),
        P("section", None),
        P("section", None, None),
        P("section", None, None),
        P("section", None),
        P("dom", None, None),
        P("dom", None),
        P("dom", None),
        P("dom", None),
    )
    return jax.shard_map(
        functools.partial(local, mesh.shape["section"], mesh.shape["dom"]),
        mesh=mesh,
        in_specs=placed,
        out_specs=(P("section", "dom", None), P("section", "dom", None)),
        check_vma=False,
    )
```

```python
import functools

import jax
import jax.numpy as jnp
from jax import lax
from jax.experimental import pallas as pl
from jax.experimental.pallas import tpu as pltpu
from jax.sharding import PartitionSpec as P

OFFSETS = (1, -1, 2, -2)
EPSILON = 1e-05
MESH = pl.DeviceIdType.MESH
BF16 = jnp.bfloat16
F32 = jnp.float32
B = 128
ROWS = 256


def product(left, right):
    return jnp.dot(left, right, preferred_element_type=F32)


def layer_norm(values, gain):
    centred = values - jnp.mean(values, axis=-1, keepdims=True)
    spread = jnp.mean(centred * centred, axis=-1, keepdims=True)
    return centred * lax.rsqrt(spread + EPSILON) * gain


def blocks_of(step):
    return pl.ds(step * (ROWS // B), ROWS // B)


def flat(blocks):
    return blocks.reshape(blocks.shape[0] * blocks.shape[1], blocks.shape[2])


def split(rows):
    return rows.reshape(rows.shape[0] // B, B, rows.shape[1])


def rows_of(step, size=ROWS):
    return pl.ds(pl.multiple_of(step * size, size), size)


def kernel(
    n_sec, n_dom,
    nl, el, en, ee, wef_h, wes_h, ge, wnf_h, wns_h, gn, pairs, sends, snd_h, rcv_h,
    fn, fe,
    x0, e0, x1, e1, xo, eo, xf, ef, wef, wes, wnf, wns, snd, rcv,
    gsr, scat, look, pr, ew, xn, msg, own,
    stage0, stage1, inc0, inc1, part0, part1, ret0, ret1,
    go_sem, load_sem, ent_sem, out_sem_x, out_sem_e,
    a_send, a_recv, c_send, c_recv, x_send, x_recv, e_send, e_recv,
):
    D = x0.shape[2]
    nb = x0.shape[0]
    kb = e0.shape[0] // B
    x_steps = x0.shape[0] * B // ROWS
    e_steps = e0.shape[0] // ROWS
    sec = lax.axis_index("section")
    dom = lax.axis_index("dom")
    nxt = lax.rem(sec + 1, n_sec)
    prv = lax.rem(sec + n_sec - 1, n_sec)
    ahead = lax.rem(sec, 2) == 1
    early = e_steps // 2

    loads = {}
    for i, (name, src, dst) in enumerate((
        ("x", nl, x0), ("snd", snd_h, snd), ("rcv", rcv_h, rcv), ("wef", wef_h.at[0], wef),
        ("e", el.at[0], e0), ("wes", wes_h.at[0], wes), ("wnf", wnf_h.at[0], wnf), ("wns", wns_h.at[0], wns),
    )):
        loads[name] = pltpu.make_async_copy(src, dst, load_sem.at[i])
    enter_x = pltpu.make_async_copy(en, x1, ent_sem.at[0])
    enter_e = pltpu.make_async_copy(ee, e1, ent_sem.at[1])
    loads["x"].start()

    barrier = pltpu.get_barrier_semaphore()
    for o in OFFSETS:
        pl.semaphore_signal(barrier, inc=1, device_id=(sec, lax.rem(dom + o + n_dom, n_dom)), device_id_type=MESH)
    pl.semaphore_signal(barrier, inc=1, device_id=(nxt, dom), device_id_type=MESH)
    pl.semaphore_signal(barrier, inc=1, device_id=(prv, dom), device_id_type=MESH)

    def forth(t, c):
        stage, inc = ((stage0, inc0), (stage1, inc1))[t]
        return pltpu.make_async_remote_copy(
            stage.at[c], inc.at[c], a_send.at[t, c], a_recv.at[t, c],
            device_id=(sec, lax.rem(dom + OFFSETS[c] + n_dom, n_dom)), device_id_type=MESH)

    def back(t, c):
        part, ret = ((part0, ret0), (part1, ret1))[t]
        return pltpu.make_async_remote_copy(
            part.at[c], ret.at[c], c_send.at[t, c], c_recv.at[t, c],
            device_id=(sec, lax.rem(dom - OFFSETS[c] + n_dom, n_dom)), device_id_type=MESH)

    def next_x(i):
        return pltpu.make_async_remote_copy(
            xo.at[blocks_of(i)], x1.at[blocks_of(i)], x_send.at[i], x_recv.at[i],
            device_id=(nxt, dom), device_id_type=MESH)

    def next_e(i):
        return pltpu.make_async_remote_copy(
            eo.at[rows_of(i)], e1.at[rows_of(i)], e_send.at[i], e_recv.at[i],
            device_id=(nxt, dom), device_id_type=MESH)

    def out_x(i):
        return pltpu.make_async_copy(xf.at[blocks_of(i)], fn.at[blocks_of(i)], out_sem_x.at[i])

    def out_e(i):
        return pltpu.make_async_copy(ef.at[rows_of(i)], fe.at[0, rows_of(i)], out_sem_e.at[i])

    def source(k):
        code = pairs[1, 0, k]
        return jnp.where(code == 0, pairs[2, 0, k], nb + code - 1)

    def send_blocks(t, x):
        for c in range(4):
            (stage0, stage1)[t][c] = x[sends[0, c]]
            forth(t, c).start()

    def tick(t, x, e, ready_x, ready_e):
        last = t == 1
        inc = (inc0, inc1)[t]
        part = (part0, part1)[t]
        ret = (ret0, ret1)[t]
        x_new = (xo, xf)[t]
        e_new = (eo, ef)[t]

        def pre(i, _):
            r = blocks_of(i)
            xb = flat(x[r])
            look[r] = split(product(xb, wef[D : 2 * D, :]).astype(BF16))
            pr[r] = split(product(xb, wef[2 * D :, :]).astype(BF16))
            return 0

        for i in range(x_steps):
            ready_x(i)
            if last and i == x_steps - 1:
                @pl.when(sec > 0)
                def _():
                    send_blocks(1, x1)
            pre(i, 0)
        if t == 0:
            loads["e"].wait()

            @pl.when(ahead)
            def _():
                for c in range(4):
                    forth(0, c).wait_send()
                pl.semaphore_signal(go_sem, inc=1, device_id=(sec - 1, dom), device_id_type=MESH)

            @pl.when(jnp.logical_not(ahead))
            def _():
                pl.semaphore_wait(go_sem, 1)
                send_blocks(0, x0)

        def edge_pre(i, _):
            ready_e(i)
            r = rows_of(i)
            ew[r, :] = product(e[r, :], wef[0:D, :])
            return 0

        lax.fori_loop(0, e_steps, edge_pre, 0, unroll=True)
        if not last:
            loads["wes"].wait()
            loads["wns"].wait()
        for c in range(4):
            forth(t, c).wait_recv()
        if not last:
            @pl.when(sec == 0)
            def _():
                enter_x.wait()
                send_blocks(1, x1)
        for c in range(0, 4, 2):
            both = flat(inc[c : c + 2])
            look[nb + c : nb + c + 2] = split(product(both, wef[D : 2 * D, :]).astype(BF16))

        def edge(i, _):
            parts = []
            for j in range(ROWS // B):
                k = i * (ROWS // B) + j
                kr = rows_of(k, B)
                src = source(k)
                rcvb = pairs[0, 0, k]
                feats = jnp.concatenate([look[src], pr[rcvb]], axis=0)
                pre_act = ew[kr, :] + product(gsr[kr, :], feats)
                parts.append(jnp.maximum(pre_act, 0.0).astype(BF16))
            r = rows_of(i)
            message = layer_norm(product(jnp.concatenate(parts, axis=0), wes[...]), ge[...])
            msg[r, :] = message.astype(BF16)
            e_new[r, :] = (e[r, :].astype(F32) + message).astype(BF16)
            if last:
                out_e(i).start()
            else:
                @pl.when(jnp.logical_and(sec < n_sec - 1, i < early))
                def _():
                    next_e(i).start()
            return 0

        lax.fori_loop(0, e_steps, edge, 0, unroll=True)
        for c in range(0, 4, 2):
            sums = product(scat[(nb + c) * B : (nb + c + 2) * B, :], msg[...]).astype(BF16)
            part[c] = sums[:B]
            part[c + 1] = sums[B:]
            back(t, c).start()
            back(t, c + 1).start()

        def own_sum(i, _):
            r = rows_of(i)
            own[r, :] = product(scat[r, :], msg[...])
            return 0

        lax.fori_loop(0, x_steps, own_sum, 0, unroll=True)
        if not last:
            loads["wnf"].wait()

        def node_pre(i, _):
            r = rows_of(i)
            xn[r, :] = product(flat(x[blocks_of(i)]), wnf[0:D, :])
            return 0

        lax.fori_loop(0, x_steps, node_pre, 0, unroll=True)
        for c in range(4):
            back(t, c).wait_recv()

        def node(i, _):
            r = rows_of(i)
            sums = []
            for j in range(ROWS // B):
                n = i * (ROWS // B) + j
                total = own[rows_of(n, B), :]
                for c in range(4):
                    total = total + jnp.where(sends[0, c] == n, 1.0, 0.0) * ret[c].astype(F32)
                sums.append(total.astype(BF16))
            agg = jnp.concatenate(sums, axis=0)
            hidden = jnp.maximum(xn[r, :] + product(agg, wnf[D:, :]), 0.0).astype(BF16)
            update = layer_norm(product(hidden, wns[...]), gn[...])
            x_new[blocks_of(i)] = split((flat(x[blocks_of(i)]).astype(F32) + update).astype(BF16))
            if last:
                out_x(i).start()
            else:
                @pl.when(sec < n_sec - 1)
                def _():
                    next_x(i).start()
            return 0

        lax.fori_loop(0, x_steps, node, 0, unroll=True)
        if not last:
            @pl.when(sec < n_sec - 1)
            def _():
                for i in range(early, e_steps):
                    next_e(i).start()

    loads["x"].wait()
    for name in ("snd", "rcv", "wef", "e", "wes", "wnf", "wns"):
        loads[name].start()

    @pl.when(sec == 0)
    def _():
        enter_x.start()
        enter_e.start()

    pl.semaphore_wait(barrier, 6)

    @pl.when(ahead)
    def _():
        send_blocks(0, x0)

    loads["snd"].wait()
    loads["rcv"].wait()

    def build(k, _):
        kr = rows_of(k, B)
        s_mat = snd[kr, :].astype(F32)
        r_mat = rcv[kr, :].astype(F32)
        gsr[kr, 0:B] = s_mat.astype(BF16)
        gsr[kr, B : 2 * B] = r_mat.astype(BF16)
        s_t = s_mat.T
        r_t = r_mat.T
        src = source(k)
        rcvb = pairs[0, 0, k]
        for n in range(nb + 4):
            block = s_t * jnp.where(src == n, 1.0, 0.0)
            if n < nb:
                block = block + r_t * jnp.where(rcvb == n, 1.0, 0.0)
            scat[n * B : (n + 1) * B, kr] = block.astype(BF16)
        return 0

    lax.fori_loop(0, kb, build, 0, unroll=2)
    loads["wef"].wait()
    tick(0, x0, e0, lambda i: None, lambda i: None)

    @pl.when(sec == 0)
    def _():
        enter_e.wait()

    def ready_x(i):
        @pl.when(sec > 0)
        def _():
            next_x(i).wait_recv()

    def ready_e(i):
        @pl.when(sec > 0)
        def _():
            next_e(i).wait_recv()

    tick(1, x1, e1, ready_x, ready_e)

    for i in range(x_steps):
        out_x(i).wait()
    for i in range(e_steps):
        out_e(i).wait()
    for c in range(4):
        forth(1, c).wait_send()
        back(0, c).wait_send()
        back(1, c).wait_send()

    @pl.when(jnp.logical_not(ahead))
    def _():
        for c in range(4):
            forth(0, c).wait_send()

    @pl.when(sec < n_sec - 1)
    def _():
        for i in range(x_steps):
            next_x(i).wait_send()
        for i in range(e_steps):
            next_e(i).wait_send()


def hand_over_kernel(nodes, edges, out_nodes, out_edges, buf, in_sem, out_sem):
    size = 2 * ROWS
    parts = [(src, dst, r) for src, dst in ((nodes, out_nodes), (edges, out_edges)) for r in range(0, src.shape[1], size)]
    reads = [
        pltpu.make_async_copy(src.at[0, pl.ds(r, size)], buf.at[i], in_sem.at[i]) for i, (src, _, r) in enumerate(parts)]
    writes = [
        pltpu.make_async_copy(buf.at[i], dst.at[0, pl.ds(r, size)], out_sem.at[i]) for i, (_, dst, r) in enumerate(parts)]
    for copy in reads:
        copy.start()
    for read, write in zip(reads, writes):
        read.wait()
        write.start()
    for copy in writes:
        copy.wait()


def hand_over(nodes, edges):
    any_space = pl.BlockSpec(memory_space=pl.ANY)
    count = (nodes.shape[1] + edges.shape[1]) // (2 * ROWS)
    return pl.pallas_call(
        hand_over_kernel,
        out_shape=(jax.ShapeDtypeStruct(nodes.shape, BF16), jax.ShapeDtypeStruct(edges.shape, BF16)),
        in_specs=[any_space] * 2,
        out_specs=(any_space,) * 2,
        scratch_shapes=[
            pltpu.VMEM((count, 2 * ROWS, nodes.shape[2]), BF16),
            pltpu.SemaphoreType.DMA((count,)), pltpu.SemaphoreType.DMA((count,))],
    )(nodes, edges)


def local(n_sec, n_dom, *args):
    nl, el = args[0], args[1]
    n_rows, D = nl.shape[1:]
    e_rows = el.shape[1]
    nb = n_rows // B
    any_space = pl.BlockSpec(memory_space=pl.ANY)
    vmem = pl.BlockSpec(memory_space=pltpu.VMEM)
    smem = pl.BlockSpec(memory_space=pltpu.SMEM)
    specs = [any_space] * 14
    specs[6] = specs[9] = vmem
    specs[10] = specs[11] = smem
    nodes = pltpu.VMEM((nb, B, D), BF16)
    edges = pltpu.VMEM((e_rows, D), BF16)
    slots = pltpu.VMEM((4, B, D), BF16)
    dma = pltpu.SemaphoreType.DMA
    x_steps, e_steps = n_rows // ROWS, e_rows // ROWS
    pairs = jnp.transpose(args[10], (2, 0, 1))
    args = (nl.reshape(nb, B, D), args[1], args[2].reshape(nb, B, D)) + args[3:10] + (pairs,) + args[11:]
    final_nodes, final_edges = pl.pallas_call(
        functools.partial(kernel, n_sec, n_dom),
        out_shape=(jax.ShapeDtypeStruct((nb, B, D), BF16), jax.ShapeDtypeStruct(el.shape, BF16)),
        in_specs=specs,
        out_specs=(any_space, any_space),
        scratch_shapes=[
            nodes, edges, nodes, edges, nodes, edges, nodes, edges,
            pltpu.VMEM((3 * D, D), BF16), pltpu.VMEM((D, D), BF16),
            pltpu.VMEM((2 * D, D), BF16), pltpu.VMEM((D, D), BF16),
            pltpu.VMEM((e_rows, B), jnp.int32), pltpu.VMEM((e_rows, B), jnp.int32),
            pltpu.VMEM((e_rows, 2 * B), BF16),
            pltpu.VMEM(((nb + 4) * B, e_rows), BF16),
            pltpu.VMEM((nb + 4, B, D), BF16),
            nodes,
            pltpu.VMEM((e_rows, D), F32),
            pltpu.VMEM((n_rows, D), F32),
            edges,
            pltpu.VMEM((n_rows, D), F32),
            slots, slots, slots, slots, slots, slots, slots, slots,
            pltpu.SemaphoreType.REGULAR, dma((8,)), dma((2,)), dma((x_steps,)), dma((e_steps,)),
            dma((2, 4)), dma((2, 4)), dma((2, 4)), dma((2, 4)),
            dma((x_steps,)), dma((x_steps,)), dma((e_steps,)), dma((e_steps,)),
        ],
        compiler_params=pltpu.CompilerParams(
            collective_id=0, has_side_effects=True, vmem_limit_bytes=56 << 20),
    )(*args)
    return hand_over(final_nodes.reshape(nl.shape), final_edges)


def solution(mesh):
    placed = (
        P("section", "dom", None),
        P("section", "dom", None),
        P("dom", None),
        P("dom", None),
        P("section", None, None),
        P("section", None, None),
        P("section", None),
        P("section", None, None),
        P("section", None, None),
        P("section", None),
        P("dom", None, None),
        P("dom", None),
        P("dom", None),
        P("dom", None),
    )
    return jax.shard_map(
        functools.partial(local, mesh.shape["section"], mesh.shape["dom"]),
        mesh=mesh,
        in_specs=placed,
        out_specs=(P("section", "dom", None), P("section", "dom", None)),
        check_vma=False,
    )
```

```python
import functools

import jax
import jax.numpy as jnp
from jax import lax
from jax.experimental import pallas as pl
from jax.experimental.pallas import tpu as pltpu
from jax.sharding import PartitionSpec as P

OFFSETS = (1, -1, 2, -2)
EPSILON = 1e-05
MESH = pl.DeviceIdType.MESH
BF16 = jnp.bfloat16
F32 = jnp.float32
B = 128
ROWS = 256


def product(left, right):
    return jnp.dot(left, right, preferred_element_type=F32)


def layer_norm(values, gain):
    centred = values - jnp.mean(values, axis=-1, keepdims=True)
    spread = jnp.mean(centred * centred, axis=-1, keepdims=True)
    return centred * lax.rsqrt(spread + EPSILON) * gain


def blocks_of(step):
    return pl.ds(step * (ROWS // B), ROWS // B)


def flat(blocks):
    return blocks.reshape(blocks.shape[0] * blocks.shape[1], blocks.shape[2])


def split(rows):
    return rows.reshape(rows.shape[0] // B, B, rows.shape[1])


def rows_of(step, size=ROWS):
    return pl.ds(pl.multiple_of(step * size, size), size)


def kernel(
    n_sec, n_dom,
    nl, el, en, ee, wef_h, wes_h, ge, wnf_h, wns_h, gn, pairs, sends, snd_h, rcv_h,
    xf, ef,
    x0, e0, x1, e1, xo, eo, wef, wes, wnf, wns, snd, rcv,
    gsr, scat, look, pr, ew, xn, msg, own,
    stage0, stage1, inc0, inc1, part0, part1, ret0, ret1,
    go_sem, load_sem, ent_sem,
    a_send, a_recv, c_send, c_recv, x_send, x_recv, e_send, e_recv,
):
    D = x0.shape[2]
    nb = x0.shape[0]
    kb = e0.shape[0] // B
    x_steps = x0.shape[0] * B // ROWS
    e_steps = e0.shape[0] // ROWS
    sec = lax.axis_index("section")
    dom = lax.axis_index("dom")
    nxt = lax.rem(sec + 1, n_sec)
    prv = lax.rem(sec + n_sec - 1, n_sec)
    ahead = lax.rem(sec, 2) == 1
    early = e_steps // 2

    loads = {}
    for i, (name, src, dst) in enumerate((
        ("x", nl, x0), ("snd", snd_h, snd), ("rcv", rcv_h, rcv), ("wef", wef_h.at[0], wef),
        ("e", el.at[0], e0), ("wes", wes_h.at[0], wes), ("wnf", wnf_h.at[0], wnf), ("wns", wns_h.at[0], wns),
    )):
        loads[name] = pltpu.make_async_copy(src, dst, load_sem.at[i])
    enter_x = pltpu.make_async_copy(en, x1, ent_sem.at[0])
    enter_e = pltpu.make_async_copy(ee, e1, ent_sem.at[1])
    loads["x"].start()

    barrier = pltpu.get_barrier_semaphore()
    for o in OFFSETS:
        pl.semaphore_signal(barrier, inc=1, device_id=(sec, lax.rem(dom + o + n_dom, n_dom)), device_id_type=MESH)
    pl.semaphore_signal(barrier, inc=1, device_id=(nxt, dom), device_id_type=MESH)
    pl.semaphore_signal(barrier, inc=1, device_id=(prv, dom), device_id_type=MESH)

    def forth(t, c):
        stage, inc = ((stage0, inc0), (stage1, inc1))[t]
        return pltpu.make_async_remote_copy(
            stage.at[c], inc.at[c], a_send.at[t, c], a_recv.at[t, c],
            device_id=(sec, lax.rem(dom + OFFSETS[c] + n_dom, n_dom)), device_id_type=MESH)

    def back(t, c):
        part, ret = ((part0, ret0), (part1, ret1))[t]
        return pltpu.make_async_remote_copy(
            part.at[c], ret.at[c], c_send.at[t, c], c_recv.at[t, c],
            device_id=(sec, lax.rem(dom - OFFSETS[c] + n_dom, n_dom)), device_id_type=MESH)

    def next_x(i):
        return pltpu.make_async_remote_copy(
            xo.at[blocks_of(i)], x1.at[blocks_of(i)], x_send.at[i], x_recv.at[i],
            device_id=(nxt, dom), device_id_type=MESH)

    def next_e(i):
        return pltpu.make_async_remote_copy(
            eo.at[rows_of(i)], e1.at[rows_of(i)], e_send.at[i], e_recv.at[i],
            device_id=(nxt, dom), device_id_type=MESH)

    def source(k):
        code = pairs[1, 0, k]
        return jnp.where(code == 0, pairs[2, 0, k], nb + code - 1)

    def send_blocks(t, x):
        for c in range(4):
            (stage0, stage1)[t][c] = x[sends[0, c]]
            forth(t, c).start()

    def tick(t, x, e, ready_x, ready_e):
        last = t == 1
        inc = (inc0, inc1)[t]
        part = (part0, part1)[t]
        ret = (ret0, ret1)[t]
        x_new = (xo, xf)[t]
        e_new = (eo, ef)[t]

        def pre(i, _):
            r = blocks_of(i)
            xb = flat(x[r])
            look[r] = split(product(xb, wef[D : 2 * D, :]).astype(BF16))
            pr[r] = split(product(xb, wef[2 * D :, :]).astype(BF16))
            return 0

        for i in range(x_steps):
            ready_x(i)
            if last and i == x_steps - 1:
                @pl.when(sec > 0)
                def _():
                    send_blocks(1, x1)
            pre(i, 0)
        if t == 0:
            loads["e"].wait()

            @pl.when(ahead)
            def _():
                for c in range(4):
                    forth(0, c).wait_send()
                pl.semaphore_signal(go_sem, inc=1, device_id=(sec - 1, dom), device_id_type=MESH)

            @pl.when(jnp.logical_not(ahead))
            def _():
                pl.semaphore_wait(go_sem, 1)
                send_blocks(0, x0)

        def edge_pre(i, _):
            ready_e(i)
            r = rows_of(i)
            ew[r, :] = product(e[r, :], wef[0:D, :])
            return 0

        lax.fori_loop(0, e_steps, edge_pre, 0, unroll=True)
        if not last:
            loads["wes"].wait()
            loads["wns"].wait()
        for c in range(4):
            forth(t, c).wait_recv()
        if not last:
            @pl.when(sec == 0)
            def _():
                enter_x.wait()
                send_blocks(1, x1)
        for c in range(0, 4, 2):
            both = flat(inc[c : c + 2])
            look[nb + c : nb + c + 2] = split(product(both, wef[D : 2 * D, :]).astype(BF16))

        def edge(i):
            parts = []
            for j in range(ROWS // B):
                k = i * (ROWS // B) + j
                kr = rows_of(k, B)
                src = source(k)
                rcvb = pairs[0, 0, k]
                feats = jnp.concatenate([look[src], pr[rcvb]], axis=0)
                pre_act = ew[kr, :] + product(gsr[kr, :], feats)
                parts.append(jnp.maximum(pre_act, 0.0).astype(BF16))
            r = rows_of(i)
            message = layer_norm(product(jnp.concatenate(parts, axis=0), wes[...]), ge[...])
            msg[r, :] = message.astype(BF16)
            e_new[r, :] = (e[r, :].astype(F32) + message).astype(BF16)

        for i in range(e_steps):
            edge(i)
            if not last and i == early - 1:
                @pl.when(sec < n_sec - 1)
                def _():
                    for j in range(early):
                        next_e(j).start()
        for c in range(0, 4, 2):
            sums = product(scat[(nb + c) * B : (nb + c + 2) * B, :], msg[...]).astype(BF16)
            part[c] = sums[:B]
            part[c + 1] = sums[B:]
            back(t, c).start()
            back(t, c + 1).start()

        def own_sum(i, _):
            r = rows_of(i)
            own[r, :] = product(scat[r, :], msg[...])
            return 0

        lax.fori_loop(0, x_steps, own_sum, 0, unroll=True)
        if not last:
            loads["wnf"].wait()

        def node_pre(i, _):
            r = rows_of(i)
            xn[r, :] = product(flat(x[blocks_of(i)]), wnf[0:D, :])
            return 0

        lax.fori_loop(0, x_steps, node_pre, 0, unroll=True)
        for c in range(4):
            back(t, c).wait_recv()

        def node(i):
            r = rows_of(i)
            sums = []
            for j in range(ROWS // B):
                n = i * (ROWS // B) + j
                total = own[rows_of(n, B), :]
                for c in range(4):
                    total = total + jnp.where(sends[0, c] == n, 1.0, 0.0) * ret[c].astype(F32)
                sums.append(total.astype(BF16))
            agg = jnp.concatenate(sums, axis=0)
            hidden = jnp.maximum(xn[r, :] + product(agg, wnf[D:, :]), 0.0).astype(BF16)
            update = layer_norm(product(hidden, wns[...]), gn[...])
            x_new[blocks_of(i)] = split((flat(x[blocks_of(i)]).astype(F32) + update).astype(BF16))

        for i in range(x_steps):
            node(i)
            if not last and i % 2 == 1:
                @pl.when(sec < n_sec - 1)
                def _():
                    next_x(i - 1).start()
                    next_x(i).start()
        if not last:
            @pl.when(sec < n_sec - 1)
            def _():
                for i in range(early, e_steps):
                    next_e(i).start()

    loads["x"].wait()
    for name in ("snd", "rcv", "wef", "e", "wes", "wnf", "wns"):
        loads[name].start()

    @pl.when(sec == 0)
    def _():
        enter_x.start()
        enter_e.start()

    pl.semaphore_wait(barrier, 6)

    @pl.when(ahead)
    def _():
        send_blocks(0, x0)

    loads["snd"].wait()
    loads["rcv"].wait()

    def build(k, _):
        kr = rows_of(k, B)
        s_mat = snd[kr, :].astype(F32)
        r_mat = rcv[kr, :].astype(F32)
        gsr[kr, 0:B] = s_mat.astype(BF16)
        gsr[kr, B : 2 * B] = r_mat.astype(BF16)
        s_t = s_mat.T
        r_t = r_mat.T
        src = source(k)
        rcvb = pairs[0, 0, k]
        for n in range(nb + 4):
            block = s_t * jnp.where(src == n, 1.0, 0.0)
            if n < nb:
                block = block + r_t * jnp.where(rcvb == n, 1.0, 0.0)
            scat[n * B : (n + 1) * B, kr] = block.astype(BF16)
        return 0

    lax.fori_loop(0, kb, build, 0, unroll=2)
    loads["wef"].wait()
    tick(0, x0, e0, lambda i: None, lambda i: None)

    @pl.when(sec == 0)
    def _():
        enter_e.wait()

    def ready_x(i):
        @pl.when(sec > 0)
        def _():
            next_x(i).wait_recv()

    def ready_e(i):
        @pl.when(sec > 0)
        def _():
            next_e(i).wait_recv()

    tick(1, x1, e1, ready_x, ready_e)

    for c in range(4):
        forth(1, c).wait_send()
        back(0, c).wait_send()
        back(1, c).wait_send()

    @pl.when(jnp.logical_not(ahead))
    def _():
        for c in range(4):
            forth(0, c).wait_send()

    @pl.when(sec < n_sec - 1)
    def _():
        for i in range(x_steps):
            next_x(i).wait_send()
        for i in range(e_steps):
            next_e(i).wait_send()


def local(n_sec, n_dom, *args):
    nl, el = args[0], args[1]
    n_rows, D = nl.shape[1:]
    e_rows = el.shape[1]
    nb = n_rows // B
    any_space = pl.BlockSpec(memory_space=pl.ANY)
    vmem = pl.BlockSpec(memory_space=pltpu.VMEM)
    smem = pl.BlockSpec(memory_space=pltpu.SMEM)
    specs = [any_space] * 14
    specs[6] = specs[9] = vmem
    specs[10] = specs[11] = smem
    nodes = pltpu.VMEM((nb, B, D), BF16)
    edges = pltpu.VMEM((e_rows, D), BF16)
    slots = pltpu.VMEM((4, B, D), BF16)
    dma = pltpu.SemaphoreType.DMA
    x_steps, e_steps = n_rows // ROWS, e_rows // ROWS
    pairs = jnp.transpose(args[10], (2, 0, 1))
    args = (nl.reshape(nb, B, D), args[1], args[2].reshape(nb, B, D)) + args[3:10] + (pairs,) + args[11:]
    final_nodes, final_edges = pl.pallas_call(
        functools.partial(kernel, n_sec, n_dom),
        out_shape=(pltpu.VMEM((nb, B, D), BF16), pltpu.VMEM((e_rows, D), BF16)),
        in_specs=specs,
        out_specs=(vmem, vmem),
        scratch_shapes=[
            nodes, edges, nodes, edges, nodes, edges,
            pltpu.VMEM((3 * D, D), BF16), pltpu.VMEM((D, D), BF16),
            pltpu.VMEM((2 * D, D), BF16), pltpu.VMEM((D, D), BF16),
            pltpu.VMEM((e_rows, B), jnp.int32), pltpu.VMEM((e_rows, B), jnp.int32),
            pltpu.VMEM((e_rows, 2 * B), BF16),
            pltpu.VMEM(((nb + 4) * B, e_rows), BF16),
            pltpu.VMEM((nb + 4, B, D), BF16),
            nodes,
            pltpu.VMEM((e_rows, D), F32),
            pltpu.VMEM((n_rows, D), F32),
            edges,
            pltpu.VMEM((n_rows, D), F32),
            slots, slots, slots, slots, slots, slots, slots, slots,
            pltpu.SemaphoreType.REGULAR, dma((8,)), dma((2,)),
            dma((2, 4)), dma((2, 4)), dma((2, 4)), dma((2, 4)),
            dma((x_steps,)), dma((x_steps,)), dma((e_steps,)), dma((e_steps,)),
        ],
        compiler_params=pltpu.CompilerParams(
            collective_id=0, has_side_effects=True, vmem_limit_bytes=56 << 20),
    )(*args)
    return final_nodes.reshape(nl.shape), final_edges.reshape(el.shape)


def solution(mesh):
    placed = (
        P("section", "dom", None),
        P("section", "dom", None),
        P("dom", None),
        P("dom", None),
        P("section", None, None),
        P("section", None, None),
        P("section", None),
        P("section", None, None),
        P("section", None, None),
        P("section", None),
        P("dom", None, None),
        P("dom", None),
        P("dom", None),
        P("dom", None),
    )
    return jax.shard_map(
        functools.partial(local, mesh.shape["section"], mesh.shape["dom"]),
        mesh=mesh,
        in_specs=placed,
        out_specs=(P("section", "dom", None), P("section", "dom", None)),
        check_vma=False,
    )
```

```python
import functools

import jax
import jax.numpy as jnp
from jax import lax
from jax.experimental import pallas as pl
from jax.experimental.pallas import tpu as pltpu
from jax.sharding import PartitionSpec as P

OFFSETS = (1, -1, 2, -2)
EPSILON = 1e-05
MESH = pl.DeviceIdType.MESH
BF16 = jnp.bfloat16
F32 = jnp.float32
B = 128
ROWS = 256


def product(left, right):
    return jnp.dot(left, right, preferred_element_type=F32)


def layer_norm(values, gain):
    centred = values - jnp.mean(values, axis=-1, keepdims=True)
    spread = jnp.mean(centred * centred, axis=-1, keepdims=True)
    return centred * lax.rsqrt(spread + EPSILON) * gain


def blocks_of(step):
    return pl.ds(step * (ROWS // B), ROWS // B)


def flat(blocks):
    return blocks.reshape(blocks.shape[0] * blocks.shape[1], blocks.shape[2])


def split(rows):
    return rows.reshape(rows.shape[0] // B, B, rows.shape[1])


def rows_of(step, size=ROWS):
    return pl.ds(pl.multiple_of(step * size, size), size)


def kernel(
    n_sec, n_dom,
    nl, el, en, ee, wef_h, wes_h, ge, wnf_h, wns_h, gn, pairs, sends, snd_h, rcv_h,
    xf, ef,
    x0, e0, x1, e1, xo, eo, wef, wes, wnf, wns, snd, rcv,
    gsr, scat, look, pr, ew, xn, msg, own,
    stage0, stage1, inc0, inc1, part0, part1, ret0, ret1,
    go_sem, load_sem, ent_sem,
    a_send, a_recv, c_send, c_recv, x_send, x_recv, e_send, e_recv,
):
    D = x0.shape[2]
    nb = x0.shape[0]
    kb = e0.shape[0] // B
    x_steps = x0.shape[0] * B // ROWS
    e_steps = e0.shape[0] // ROWS
    sec = lax.axis_index("section")
    dom = lax.axis_index("dom")
    nxt = lax.rem(sec + 1, n_sec)
    prv = lax.rem(sec + n_sec - 1, n_sec)
    ahead = lax.rem(sec, 2) == 1
    early = e_steps // 2

    loads = {}
    for i, (name, src, dst) in enumerate((
        ("x", nl, x0), ("snd", snd_h, snd), ("rcv", rcv_h, rcv), ("wef", wef_h.at[0], wef),
        ("e", el.at[0], e0), ("wes", wes_h.at[0], wes), ("wnf", wnf_h.at[0], wnf), ("wns", wns_h.at[0], wns),
    )):
        loads[name] = pltpu.make_async_copy(src, dst, load_sem.at[i])
    enter_x = pltpu.make_async_copy(en, x1, ent_sem.at[0])
    enter_e = pltpu.make_async_copy(ee, e1, ent_sem.at[1])
    loads["x"].start()

    barrier = pltpu.get_barrier_semaphore()
    for o in OFFSETS:
        pl.semaphore_signal(barrier, inc=1, device_id=(sec, lax.rem(dom + o + n_dom, n_dom)), device_id_type=MESH)
    pl.semaphore_signal(barrier, inc=1, device_id=(nxt, dom), device_id_type=MESH)
    pl.semaphore_signal(barrier, inc=1, device_id=(prv, dom), device_id_type=MESH)

    def forth(t, c):
        stage, inc = ((stage0, inc0), (stage1, inc1))[t]
        return pltpu.make_async_remote_copy(
            stage.at[c], inc.at[c], a_send.at[t, c], a_recv.at[t, c],
            device_id=(sec, lax.rem(dom + OFFSETS[c] + n_dom, n_dom)), device_id_type=MESH)

    def back(t, c):
        part, ret = ((part0, ret0), (part1, ret1))[t]
        return pltpu.make_async_remote_copy(
            part.at[c], ret.at[c], c_send.at[t, c], c_recv.at[t, c],
            device_id=(sec, lax.rem(dom - OFFSETS[c] + n_dom, n_dom)), device_id_type=MESH)

    def next_x(i):
        return pltpu.make_async_remote_copy(
            xo.at[blocks_of(i)], x1.at[blocks_of(i)], x_send.at[i], x_recv.at[i],
            device_id=(nxt, dom), device_id_type=MESH)

    def next_e(i):
        return pltpu.make_async_remote_copy(
            eo.at[rows_of(i)], e1.at[rows_of(i)], e_send.at[i], e_recv.at[i],
            device_id=(nxt, dom), device_id_type=MESH)

    def source(k):
        code = pairs[1, 0, k]
        return jnp.where(code == 0, pairs[2, 0, k], nb + code - 1)

    def send_blocks(t, x):
        for c in range(4):
            (stage0, stage1)[t][c] = x[sends[0, c]]
            forth(t, c).start()

    def tick(t, x, e, ready_x, ready_e):
        last = t == 1
        inc = (inc0, inc1)[t]
        part = (part0, part1)[t]
        ret = (ret0, ret1)[t]
        x_new = (xo, xf)[t]
        e_new = (eo, ef)[t]

        def pre(i, _):
            r = blocks_of(i)
            xb = flat(x[r])
            look[r] = split(product(xb, wef[D : 2 * D, :]).astype(BF16))
            pr[r] = split(product(xb, wef[2 * D :, :]).astype(BF16))
            return 0

        for i in range(x_steps):
            ready_x(i)
            if last and i == x_steps - 1:
                @pl.when(sec > 0)
                def _():
                    send_blocks(1, x1)
            pre(i, 0)
        if t == 0:
            loads["e"].wait()

            @pl.when(ahead)
            def _():
                for c in range(4):
                    forth(0, c).wait_send()
                pl.semaphore_signal(go_sem, inc=1, device_id=(sec - 1, dom), device_id_type=MESH)

            @pl.when(jnp.logical_not(ahead))
            def _():
                pl.semaphore_wait(go_sem, 1)
                send_blocks(0, x0)

        if last:
            @pl.when(sec < n_sec - 1)
            def _():
                for i in range(x_steps):
                    next_x(i).wait_send()
                for i in range(early, e_steps):
                    next_e(i).start()

        def edge_pre(i, _):
            ready_e(i)
            r = rows_of(i)
            ew[r, :] = product(e[r, :], wef[0:D, :])
            return 0

        lax.fori_loop(0, e_steps, edge_pre, 0, unroll=True)
        if not last:
            loads["wes"].wait()
            loads["wns"].wait()
        for c in range(4):
            forth(t, c).wait_recv()
        for c in range(0, 4, 2):
            both = flat(inc[c : c + 2])
            look[nb + c : nb + c + 2] = split(product(both, wef[D : 2 * D, :]).astype(BF16))

        def edge(i):
            parts = []
            for j in range(ROWS // B):
                k = i * (ROWS // B) + j
                kr = rows_of(k, B)
                src = source(k)
                rcvb = pairs[0, 0, k]
                feats = jnp.concatenate([look[src], pr[rcvb]], axis=0)
                pre_act = ew[kr, :] + product(gsr[kr, :], feats)
                parts.append(jnp.maximum(pre_act, 0.0).astype(BF16))
            r = rows_of(i)
            message = layer_norm(product(jnp.concatenate(parts, axis=0), wes[...]), ge[...])
            msg[r, :] = message.astype(BF16)
            e_new[r, :] = (e[r, :].astype(F32) + message).astype(BF16)

        for i in range(e_steps):
            edge(i)
            if not last and i == early - 1:
                @pl.when(sec < n_sec - 1)
                def _():
                    for j in range(early):
                        next_e(j).start()
        for c in range(0, 4, 2):
            sums = product(scat[(nb + c) * B : (nb + c + 2) * B, :], msg[...]).astype(BF16)
            part[c] = sums[:B]
            part[c + 1] = sums[B:]
            back(t, c).start()
            back(t, c + 1).start()

        def own_sum(i, _):
            r = rows_of(i)
            own[r, :] = product(scat[r, :], msg[...])
            return 0

        lax.fori_loop(0, x_steps, own_sum, 0, unroll=True)
        if not last:
            loads["wnf"].wait()

        def node_pre(i, _):
            r = rows_of(i)
            xn[r, :] = product(flat(x[blocks_of(i)]), wnf[0:D, :])
            return 0

        lax.fori_loop(0, x_steps, node_pre, 0, unroll=True)
        for c in range(4):
            back(t, c).wait_recv()
        if not last:
            @pl.when(sec == 0)
            def _():
                enter_x.wait()
                send_blocks(1, x1)

        def node(i):
            r = rows_of(i)
            sums = []
            for j in range(ROWS // B):
                n = i * (ROWS // B) + j
                total = own[rows_of(n, B), :]
                for c in range(4):
                    total = total + jnp.where(sends[0, c] == n, 1.0, 0.0) * ret[c].astype(F32)
                sums.append(total.astype(BF16))
            agg = jnp.concatenate(sums, axis=0)
            hidden = jnp.maximum(xn[r, :] + product(agg, wnf[D:, :]), 0.0).astype(BF16)
            update = layer_norm(product(hidden, wns[...]), gn[...])
            x_new[blocks_of(i)] = split((flat(x[blocks_of(i)]).astype(F32) + update).astype(BF16))

        for i in range(x_steps):
            node(i)
            if not last and i in (0, x_steps - 1):
                @pl.when(sec < n_sec - 1)
                def _():
                    for j in range(min(i, 1), i + 1):
                        next_x(j).start()

    loads["x"].wait()
    for name in ("snd", "rcv", "wef", "e", "wes", "wnf", "wns"):
        loads[name].start()

    @pl.when(sec == 0)
    def _():
        enter_x.start()
        enter_e.start()

    pl.semaphore_wait(barrier, 6)

    @pl.when(ahead)
    def _():
        send_blocks(0, x0)

    loads["snd"].wait()
    loads["rcv"].wait()

    def build(k, _):
        kr = rows_of(k, B)
        s_mat = snd[kr, :].astype(F32)
        r_mat = rcv[kr, :].astype(F32)
        gsr[kr, 0:B] = s_mat.astype(BF16)
        gsr[kr, B : 2 * B] = r_mat.astype(BF16)
        s_t = s_mat.T
        r_t = r_mat.T
        src = source(k)
        rcvb = pairs[0, 0, k]
        for n in range(nb + 4):
            block = s_t * jnp.where(src == n, 1.0, 0.0)
            if n < nb:
                block = block + r_t * jnp.where(rcvb == n, 1.0, 0.0)
            scat[n * B : (n + 1) * B, kr] = block.astype(BF16)
        return 0

    lax.fori_loop(0, kb, build, 0, unroll=2)
    loads["wef"].wait()
    tick(0, x0, e0, lambda i: None, lambda i: None)

    @pl.when(sec == 0)
    def _():
        enter_e.wait()

    def ready_x(i):
        @pl.when(sec > 0)
        def _():
            next_x(i).wait_recv()

    def ready_e(i):
        @pl.when(sec > 0)
        def _():
            next_e(i).wait_recv()

    tick(1, x1, e1, ready_x, ready_e)

    for c in range(4):
        forth(1, c).wait_send()
        back(0, c).wait_send()
        back(1, c).wait_send()

    @pl.when(jnp.logical_not(ahead))
    def _():
        for c in range(4):
            forth(0, c).wait_send()

    @pl.when(sec < n_sec - 1)
    def _():
        for i in range(e_steps):
            next_e(i).wait_send()


def local(n_sec, n_dom, *args):
    nl, el = args[0], args[1]
    n_rows, D = nl.shape[1:]
    e_rows = el.shape[1]
    nb = n_rows // B
    any_space = pl.BlockSpec(memory_space=pl.ANY)
    vmem = pl.BlockSpec(memory_space=pltpu.VMEM)
    smem = pl.BlockSpec(memory_space=pltpu.SMEM)
    specs = [any_space] * 14
    specs[6] = specs[9] = vmem
    specs[10] = specs[11] = smem
    nodes = pltpu.VMEM((nb, B, D), BF16)
    edges = pltpu.VMEM((e_rows, D), BF16)
    slots = pltpu.VMEM((4, B, D), BF16)
    dma = pltpu.SemaphoreType.DMA
    x_steps, e_steps = n_rows // ROWS, e_rows // ROWS
    pairs = jnp.transpose(args[10], (2, 0, 1))
    args = (nl.reshape(nb, B, D), args[1], args[2].reshape(nb, B, D)) + args[3:10] + (pairs,) + args[11:]
    final_nodes, final_edges = pl.pallas_call(
        functools.partial(kernel, n_sec, n_dom),
        out_shape=(pltpu.VMEM((nb, B, D), BF16), pltpu.VMEM((e_rows, D), BF16)),
        in_specs=specs,
        out_specs=(vmem, vmem),
        scratch_shapes=[
            nodes, edges, nodes, edges, nodes, edges,
            pltpu.VMEM((3 * D, D), BF16), pltpu.VMEM((D, D), BF16),
            pltpu.VMEM((2 * D, D), BF16), pltpu.VMEM((D, D), BF16),
            pltpu.VMEM((e_rows, B), jnp.int32), pltpu.VMEM((e_rows, B), jnp.int32),
            pltpu.VMEM((e_rows, 2 * B), BF16),
            pltpu.VMEM(((nb + 4) * B, e_rows), BF16),
            pltpu.VMEM((nb + 4, B, D), BF16),
            nodes,
            pltpu.VMEM((e_rows, D), F32),
            pltpu.VMEM((n_rows, D), F32),
            edges,
            pltpu.VMEM((n_rows, D), F32),
            slots, slots, slots, slots, slots, slots, slots, slots,
            pltpu.SemaphoreType.REGULAR, dma((8,)), dma((2,)),
            dma((2, 4)), dma((2, 4)), dma((2, 4)), dma((2, 4)),
            dma((x_steps,)), dma((x_steps,)), dma((e_steps,)), dma((e_steps,)),
        ],
        compiler_params=pltpu.CompilerParams(
            collective_id=0, has_side_effects=True, vmem_limit_bytes=56 << 20),
    )(*args)
    return final_nodes.reshape(nl.shape), final_edges.reshape(el.shape)


def solution(mesh):
    placed = (
        P("section", "dom", None),
        P("section", "dom", None),
        P("dom", None),
        P("dom", None),
        P("section", None, None),
        P("section", None, None),
        P("section", None),
        P("section", None, None),
        P("section", None, None),
        P("section", None),
        P("dom", None, None),
        P("dom", None),
        P("dom", None),
        P("dom", None),
    )
    return jax.shard_map(
        functools.partial(local, mesh.shape["section"], mesh.shape["dom"]),
        mesh=mesh,
        in_specs=placed,
        out_specs=(P("section", "dom", None), P("section", "dom", None)),
        check_vma=False,
    )
```

```python
import functools

import jax
import jax.numpy as jnp
from jax import lax
from jax.experimental import pallas as pl
from jax.experimental.pallas import tpu as pltpu
from jax.sharding import PartitionSpec as P

OFFSETS = (1, -1, 2, -2)
EPSILON = 1e-05
MESH = pl.DeviceIdType.MESH
BF16 = jnp.bfloat16
F32 = jnp.float32
B = 128
ROWS = 256


def product(left, right):
    return jnp.dot(left, right, preferred_element_type=F32)


def layer_norm(values, gain):
    centred = values - jnp.mean(values, axis=-1, keepdims=True)
    spread = jnp.mean(centred * centred, axis=-1, keepdims=True)
    return centred * lax.rsqrt(spread + EPSILON) * gain


def blocks_of(step):
    return pl.ds(step * (ROWS // B), ROWS // B)


def flat(blocks):
    return blocks.reshape(blocks.shape[0] * blocks.shape[1], blocks.shape[2])


def split(rows):
    return rows.reshape(rows.shape[0] // B, B, rows.shape[1])


def rows_of(step, size=ROWS):
    return pl.ds(pl.multiple_of(step * size, size), size)


def kernel(
    n_sec, n_dom,
    nl, el, en, ee, wef_h, wes_h, ge, wnf_h, wns_h, gn, pairs, sends, snd_h, rcv_h,
    xf, ef,
    x0, e0, x1, e1, xo, eo, wef, wes, wnf, wns, snd, rcv,
    gsr, scat, look, pr, ew, xn, msg, own,
    stage0, stage1, inc0, inc1, part0, part1, ret0, ret1,
    go_sem, load_sem, ent_sem,
    a_send, a_recv, c_send, c_recv, x_send, x_recv, e_send, e_recv,
):
    D = x0.shape[2]
    nb = x0.shape[0]
    kb = e0.shape[0] // B
    x_steps = x0.shape[0] * B // ROWS
    e_steps = e0.shape[0] // ROWS
    sec = lax.axis_index("section")
    dom = lax.axis_index("dom")
    nxt = lax.rem(sec + 1, n_sec)
    prv = lax.rem(sec + n_sec - 1, n_sec)
    ahead = lax.rem(sec, 2) == 1
    early = e_steps // 2

    loads = {}
    for i, (name, src, dst) in enumerate((
        ("x", nl, x0), ("snd", snd_h, snd), ("rcv", rcv_h, rcv), ("wef", wef_h.at[0], wef),
        ("e", el.at[0], e0), ("wes", wes_h.at[0], wes), ("wnf", wnf_h.at[0], wnf), ("wns", wns_h.at[0], wns),
    )):
        loads[name] = pltpu.make_async_copy(src, dst, load_sem.at[i])
    enter_x = pltpu.make_async_copy(en, x1, ent_sem.at[0])
    enter_e = pltpu.make_async_copy(ee, e1, ent_sem.at[1])
    loads["x"].start()

    barrier = pltpu.get_barrier_semaphore()
    for o in OFFSETS:
        pl.semaphore_signal(barrier, inc=1, device_id=(sec, lax.rem(dom + o + n_dom, n_dom)), device_id_type=MESH)
    pl.semaphore_signal(barrier, inc=1, device_id=(nxt, dom), device_id_type=MESH)
    pl.semaphore_signal(barrier, inc=1, device_id=(prv, dom), device_id_type=MESH)

    def forth(t, c):
        stage, inc = ((stage0, inc0), (stage1, inc1))[t]
        return pltpu.make_async_remote_copy(
            stage.at[c], inc.at[c], a_send.at[t, c], a_recv.at[t, c],
            device_id=(sec, lax.rem(dom + OFFSETS[c] + n_dom, n_dom)), device_id_type=MESH)

    def back(t, c):
        part, ret = ((part0, ret0), (part1, ret1))[t]
        return pltpu.make_async_remote_copy(
            part.at[c], ret.at[c], c_send.at[t, c], c_recv.at[t, c],
            device_id=(sec, lax.rem(dom - OFFSETS[c] + n_dom, n_dom)), device_id_type=MESH)

    def next_x(i):
        return pltpu.make_async_remote_copy(
            xo.at[blocks_of(i)], x1.at[blocks_of(i)], x_send.at[i], x_recv.at[i],
            device_id=(nxt, dom), device_id_type=MESH)

    def next_e(i):
        return pltpu.make_async_remote_copy(
            eo.at[rows_of(i)], e1.at[rows_of(i)], e_send.at[i], e_recv.at[i],
            device_id=(nxt, dom), device_id_type=MESH)

    def source(k):
        code = pairs[1, 0, k]
        return jnp.where(code == 0, pairs[2, 0, k], nb + code - 1)

    def send_blocks(t, x):
        for c in range(4):
            (stage0, stage1)[t][c] = x[sends[0, c]]
            forth(t, c).start()

    def tick(t, x, e, ready_x, ready_e):
        last = t == 1
        inc = (inc0, inc1)[t]
        part = (part0, part1)[t]
        ret = (ret0, ret1)[t]
        x_new = (xo, xf)[t]
        e_new = (eo, ef)[t]

        def pre(i, _):
            r = blocks_of(i)
            xb = flat(x[r])
            look[r] = split(product(xb, wef[D : 2 * D, :]).astype(BF16))
            pr[r] = split(product(xb, wef[2 * D :, :]).astype(BF16))
            return 0

        for i in range(x_steps):
            ready_x(i)
            if last and i == x_steps - 1:
                @pl.when(sec > 0)
                def _():
                    send_blocks(1, x1)
            pre(i, 0)
        if t == 0:
            loads["e"].wait()

            @pl.when(ahead)
            def _():
                for c in range(4):
                    forth(0, c).wait_send()
                pl.semaphore_signal(go_sem, inc=1, device_id=(sec - 1, dom), device_id_type=MESH)

            @pl.when(jnp.logical_not(ahead))
            def _():
                pl.semaphore_wait(go_sem, 1)
                send_blocks(0, x0)

        if last:
            @pl.when(sec < n_sec - 1)
            def _():
                for i in range(x_steps):
                    next_x(i).wait_send()
                for i in range(early, e_steps):
                    next_e(i).start()

        def edge_pre(i, _):
            ready_e(i)
            r = rows_of(i)
            ew[r, :] = product(e[r, :], wef[0:D, :])
            return 0

        lax.fori_loop(0, e_steps, edge_pre, 0, unroll=True)
        if not last:
            loads["wes"].wait()
            loads["wns"].wait()
        for c in range(0, 4, 2):
            forth(t, c).wait_recv()
            forth(t, c + 1).wait_recv()
            both = flat(inc[c : c + 2])
            look[nb + c : nb + c + 2] = split(product(both, wef[D : 2 * D, :]).astype(BF16))

        def edge(i):
            parts = []
            for j in range(ROWS // B):
                k = i * (ROWS // B) + j
                kr = rows_of(k, B)
                src = source(k)
                rcvb = pairs[0, 0, k]
                feats = jnp.concatenate([look[src], pr[rcvb]], axis=0)
                pre_act = ew[kr, :] + product(gsr[kr, :], feats)
                parts.append(jnp.maximum(pre_act, 0.0).astype(BF16))
            r = rows_of(i)
            message = layer_norm(product(jnp.concatenate(parts, axis=0), wes[...]), ge[...])
            msg[r, :] = message.astype(BF16)
            e_new[r, :] = (e[r, :].astype(F32) + message).astype(BF16)

        for i in range(e_steps):
            edge(i)
            if not last and i == early - 1:
                @pl.when(sec < n_sec - 1)
                def _():
                    for j in range(early):
                        next_e(j).start()
        for c in (2, 0):
            sums = product(scat[(nb + c) * B : (nb + c + 2) * B, :], msg[...]).astype(BF16)
            part[c] = sums[:B]
            part[c + 1] = sums[B:]
            back(t, c).start()
            back(t, c + 1).start()

        def own_sum(i, _):
            r = rows_of(i)
            own[r, :] = product(scat[r, :], msg[...])
            return 0

        lax.fori_loop(0, x_steps, own_sum, 0, unroll=True)
        if not last:
            loads["wnf"].wait()

        def node_pre(i, _):
            r = rows_of(i)
            xn[r, :] = product(flat(x[blocks_of(i)]), wnf[0:D, :])
            return 0

        lax.fori_loop(0, x_steps, node_pre, 0, unroll=True)
        for c in range(4):
            back(t, c).wait_recv()
        if not last:
            @pl.when(sec == 0)
            def _():
                enter_x.wait()
                send_blocks(1, x1)

        def node(i):
            r = rows_of(i)
            sums = []
            for j in range(ROWS // B):
                n = i * (ROWS // B) + j
                total = own[rows_of(n, B), :]
                for c in range(4):
                    total = total + jnp.where(sends[0, c] == n, 1.0, 0.0) * ret[c].astype(F32)
                sums.append(total.astype(BF16))
            agg = jnp.concatenate(sums, axis=0)
            hidden = jnp.maximum(xn[r, :] + product(agg, wnf[D:, :]), 0.0).astype(BF16)
            update = layer_norm(product(hidden, wns[...]), gn[...])
            x_new[blocks_of(i)] = split((flat(x[blocks_of(i)]).astype(F32) + update).astype(BF16))

        for i in range(x_steps):
            node(i)
            if not last and i in (0, x_steps - 1):
                @pl.when(sec < n_sec - 1)
                def _():
                    for j in range(min(i, 1), i + 1):
                        next_x(j).start()

    loads["x"].wait()
    for name in ("snd", "rcv", "wef", "e", "wes", "wnf", "wns"):
        loads[name].start()

    @pl.when(sec == 0)
    def _():
        enter_x.start()
        enter_e.start()

    pl.semaphore_wait(barrier, 6)

    @pl.when(ahead)
    def _():
        send_blocks(0, x0)

    loads["snd"].wait()
    loads["rcv"].wait()

    def build(k, _):
        kr = rows_of(k, B)
        s_mat = snd[kr, :].astype(F32)
        r_mat = rcv[kr, :].astype(F32)
        gsr[kr, 0:B] = s_mat.astype(BF16)
        gsr[kr, B : 2 * B] = r_mat.astype(BF16)
        s_t = s_mat.T
        r_t = r_mat.T
        src = source(k)
        rcvb = pairs[0, 0, k]
        for n in range(nb + 4):
            block = s_t * jnp.where(src == n, 1.0, 0.0)
            if n < nb:
                block = block + r_t * jnp.where(rcvb == n, 1.0, 0.0)
            scat[n * B : (n + 1) * B, kr] = block.astype(BF16)
        return 0

    lax.fori_loop(0, kb, build, 0, unroll=2)
    loads["wef"].wait()
    tick(0, x0, e0, lambda i: None, lambda i: None)

    @pl.when(sec == 0)
    def _():
        enter_e.wait()

    def ready_x(i):
        @pl.when(sec > 0)
        def _():
            next_x(i).wait_recv()

    def ready_e(i):
        @pl.when(sec > 0)
        def _():
            next_e(i).wait_recv()

    tick(1, x1, e1, ready_x, ready_e)

    for c in range(4):
        forth(1, c).wait_send()
        back(0, c).wait_send()
        back(1, c).wait_send()

    @pl.when(jnp.logical_not(ahead))
    def _():
        for c in range(4):
            forth(0, c).wait_send()

    @pl.when(sec < n_sec - 1)
    def _():
        for i in range(e_steps):
            next_e(i).wait_send()


def local(n_sec, n_dom, *args):
    nl, el = args[0], args[1]
    n_rows, D = nl.shape[1:]
    e_rows = el.shape[1]
    nb = n_rows // B
    any_space = pl.BlockSpec(memory_space=pl.ANY)
    vmem = pl.BlockSpec(memory_space=pltpu.VMEM)
    smem = pl.BlockSpec(memory_space=pltpu.SMEM)
    specs = [any_space] * 14
    specs[6] = specs[9] = vmem
    specs[10] = specs[11] = smem
    nodes = pltpu.VMEM((nb, B, D), BF16)
    edges = pltpu.VMEM((e_rows, D), BF16)
    slots = pltpu.VMEM((4, B, D), BF16)
    dma = pltpu.SemaphoreType.DMA
    x_steps, e_steps = n_rows // ROWS, e_rows // ROWS
    pairs = jnp.transpose(args[10], (2, 0, 1))
    args = (nl.reshape(nb, B, D), args[1], args[2].reshape(nb, B, D)) + args[3:10] + (pairs,) + args[11:]
    final_nodes, final_edges = pl.pallas_call(
        functools.partial(kernel, n_sec, n_dom),
        out_shape=(pltpu.VMEM((nb, B, D), BF16), pltpu.VMEM((e_rows, D), BF16)),
        in_specs=specs,
        out_specs=(vmem, vmem),
        scratch_shapes=[
            nodes, edges, nodes, edges, nodes, edges,
            pltpu.VMEM((3 * D, D), BF16), pltpu.VMEM((D, D), BF16),
            pltpu.VMEM((2 * D, D), BF16), pltpu.VMEM((D, D), BF16),
            pltpu.VMEM((e_rows, B), jnp.int32), pltpu.VMEM((e_rows, B), jnp.int32),
            pltpu.VMEM((e_rows, 2 * B), BF16),
            pltpu.VMEM(((nb + 4) * B, e_rows), BF16),
            pltpu.VMEM((nb + 4, B, D), BF16),
            nodes,
            pltpu.VMEM((e_rows, D), F32),
            pltpu.VMEM((n_rows, D), F32),
            edges,
            pltpu.VMEM((n_rows, D), F32),
            slots, slots, slots, slots, slots, slots, slots, slots,
            pltpu.SemaphoreType.REGULAR, dma((8,)), dma((2,)),
            dma((2, 4)), dma((2, 4)), dma((2, 4)), dma((2, 4)),
            dma((x_steps,)), dma((x_steps,)), dma((e_steps,)), dma((e_steps,)),
        ],
        compiler_params=pltpu.CompilerParams(
            collective_id=0, has_side_effects=True, vmem_limit_bytes=56 << 20),
    )(*args)
    return final_nodes.reshape(nl.shape), final_edges.reshape(el.shape)


def solution(mesh):
    placed = (
        P("section", "dom", None),
        P("section", "dom", None),
        P("dom", None),
        P("dom", None),
        P("section", None, None),
        P("section", None, None),
        P("section", None),
        P("section", None, None),
        P("section", None, None),
        P("section", None),
        P("dom", None, None),
        P("dom", None),
        P("dom", None),
        P("dom", None),
    )
    return jax.shard_map(
        functools.partial(local, mesh.shape["section"], mesh.shape["dom"]),
        mesh=mesh,
        in_specs=placed,
        out_specs=(P("section", "dom", None), P("section", "dom", None)),
        check_vma=False,
    )
```
